32 devices in a mesh: grp: 4 (over x, core), dev: 8 (over z, y).
Axes of the slice: x: 2, y: 2, z: 4, core: 2. Of those that a mesh axis runs over, the one named last changes fastest.
Arguments:
- ladder_amps: bfloat16 [16, 72, 4096], P('dev', 'grp'), may hold values from -6 to 6
- ladder_ids: int32 [16, 72], P('dev', 'grp'), may hold values from 0 to 23, as said below
- ladder_count: int32 [16, 4], P('dev', 'grp'), may hold values from 9 to 18, as said below
- cycle_amps: bfloat16 [16, 24, 4096], P('dev', 'grp'), may hold values from -6 to 6
- cycle_ids: int32 [16, 24], P('dev', 'grp'), may hold values from 0 to 7, as said below
- cycle_count: int32 [16, 4], P('dev', 'grp'), may hold values from 3 to 6, as said below
- ladder_panel: bfloat16 [6144, 4096], P('grp', 'dev'), may hold values from -0.078125 to 0.078125
- cycle_panel: bfloat16 [2048, 4096], P('grp', 'dev'), may hold values from -0.125 to 0.125
- owners: int32 [16], replicated, may hold values from 0 to 15, each once
- base: float32 [1024, 4096], P('grp', 'dev'), may hold values from -6 to 6
Outputs:
- residual: float32 [1024, 4096], P('grp', 'dev')
The draws below stay inside these ranges and needn't reach their ends.
Inputs may be any that keep to these rules, and one draw needn't show every extreme that they name: `ladder_ids`: within one row tile and group the slots name distinct tiles of 0 to 23. `cycle_ids`: within one row tile and group the slots name distinct tiles of 0 to 7. `ladder_count`: slots at or past the count are not live; in every group some row tile has all 18 slots live. `cycle_count`: slots at or past the count are not live; in every group some row tile has all 6 slots live.
All inputs are finite; a program needn't handle non-finite values.
Results may differ from the reference program's by a relative error of at most 0.0003.
Values may be sent and summed in bfloat16 or wider, within the bound.
No kernel may reach another device: no remote copies, remote signals or barrier semaphores. Data moves between devices by JAX's collectives and lax.ppermute only.
A program may use at most 128 MiB of HBM per device.

```python
import jax
import jax.numpy as jnp
from jax import lax

TS = 64
KLT = 24
KRT = 8
KCAP_L = 18
KCAP_R = 6
ROW_TILES = 16
ROWS = 1024
COLS = 4096
KL_ROWS = 6144
KR_ROWS = 2048
L_SLOTS = 72
R_SLOTS = 24
N_GRP = 4


def tile_lists(key, ktiles, cap):
    scores = jax.random.randint(key, (ROW_TILES, N_GRP, ktiles), 0, 1 << 20) * ktiles
    scores = scores + jnp.arange(ktiles, dtype=jnp.int32)[None, None, :]
    order = jnp.argsort(scores, axis=-1, stable=True)
    return order[:, :, :cap].reshape(ROW_TILES, N_GRP * cap).astype(jnp.int32)


def slot_counts(key, cap):
    first_key, second_key = jax.random.split(key)
    lower = (cap + 1) // 2
    counts = jax.random.randint(first_key, (ROW_TILES, N_GRP), lower, cap + 1)
    chosen = jax.random.randint(second_key, (1, N_GRP), 0, ROW_TILES)
    full_row = jnp.arange(ROW_TILES, dtype=jnp.int32)[:, None] == chosen
    return jnp.where(full_row, cap, counts).astype(jnp.int32)


def draw_ladder_ids(key, part):
    return tile_lists(jax.random.fold_in(key, 11), KLT, KCAP_L)


def draw_cycle_ids(key, part):
    return tile_lists(jax.random.fold_in(key, 23), KRT, KCAP_R)


def draw_ladder_count(key, part):
    return slot_counts(jax.random.fold_in(key, 37), KCAP_L)


def draw_cycle_count(key, part):
    return slot_counts(jax.random.fold_in(key, 41), KCAP_R)


def steps_of(key, extent, cuts, least, largest):
    def one(axis_at, shards_of):
        draws = jax.random.uniform(jax.random.fold_in(jax.random.fold_in(key, 6), axis_at), (shards_of,), jnp.float32, least / len(cuts), largest / len(cuts))
        return jnp.repeat(jnp.exp(draws), extent[axis_at] // shards_of).reshape((-1,) + (1,) * (len(extent) - axis_at - 1))

    loudness = one(*cuts[0])
    for cut in cuts[1:]:
        loudness = loudness * one(*cut)
    return loudness


def centred(own_key, dims, width, reach, cuts=(), held_as=jnp.bfloat16):
    gain = steps_of(own_key, dims, cuts, -0.22, 0.18) if cuts else 1.0
    drawn = jax.random.normal(own_key, dims, jnp.float32) * width * gain
    return jnp.minimum(jnp.maximum(drawn, -reach), reach).astype(held_as)


def setup_inputs(seed: int = 0) -> dict:
    arg_keys = jax.random.split(jax.random.key(seed), 11)
    ladder_amps = centred(arg_keys[0], (ROW_TILES, L_SLOTS, TS * TS), 1.0, 6.0, ((0, 8), (1, 4)))
    ladder_ids = draw_ladder_ids(jax.random.fold_in(arg_keys[10], 71), 0)
    ladder_count = draw_ladder_count(jax.random.fold_in(arg_keys[10], 71), 0)
    cycle_amps = centred(arg_keys[3], (ROW_TILES, R_SLOTS, TS * TS), 1.0, 6.0, ((0, 8), (1, 4)))
    cycle_ids = draw_cycle_ids(jax.random.fold_in(arg_keys[10], 71), 0)
    cycle_count = draw_cycle_count(jax.random.fold_in(arg_keys[10], 71), 0)
    ladder_panel = centred(arg_keys[6], (KL_ROWS, COLS), KL_ROWS ** -0.5, 0.078125, ((0, 4), (1, 8)))
    cycle_panel = centred(arg_keys[7], (KR_ROWS, COLS), KR_ROWS ** -0.5, 0.125, ((0, 4), (1, 8)))
    owners = jax.random.permutation(arg_keys[8], ROW_TILES).astype(jnp.int32)
    base = centred(arg_keys[9], (ROWS, COLS), 1.0, 6.0, ((0, 4), (1, 8)), jnp.float32)
    return {"ladder_amps": ladder_amps, "ladder_ids": ladder_ids, "ladder_count": ladder_count, "cycle_amps": cycle_amps, "cycle_ids": cycle_ids, "cycle_count": cycle_count, "ladder_panel": ladder_panel, "cycle_panel": cycle_panel, "owners": owners, "base": base}


def place_tiles(amps, ids, count, group, cap, ktiles):
    block = lax.dynamic_slice_in_dim(amps, group * cap, cap, 1)
    slots = lax.dynamic_slice_in_dim(ids, group * cap, cap, 1)
    filled = lax.dynamic_slice_in_dim(count, group, 1, 1)
    live_slots = (jnp.arange(cap, dtype=jnp.int32)[None, :] < filled).astype(jnp.float32)
    onehot = (slots[:, :, None] == jnp.arange(ktiles, dtype=jnp.int32)[None, None, :]).astype(jnp.float32)
    onehot = onehot * live_slots[:, :, None]
    tiles = block.astype(jnp.float32).reshape(ROW_TILES, cap, TS, TS)
    dense = jnp.einsum("rjk,rjab->rakb", onehot, tiles)
    return dense.reshape(ROW_TILES * TS, ktiles * TS).astype(jnp.bfloat16)


def reference(ladder_amps, ladder_ids, ladder_count, cycle_amps, cycle_ids, cycle_count, ladder_panel, cycle_panel, owners, base):
    def add_group(total, group):
        ladder_dense = place_tiles(ladder_amps, ladder_ids, ladder_count, group, KCAP_L, KLT)
        cycle_dense = place_tiles(cycle_amps, cycle_ids, cycle_count, group, KCAP_R, KRT)
        ladder_rows = lax.dynamic_slice_in_dim(ladder_panel, group * (KLT * TS), KLT * TS, 0)
        cycle_rows = lax.dynamic_slice_in_dim(cycle_panel, group * (KRT * TS), KRT * TS, 0)
        part_sum = jnp.dot(ladder_dense, ladder_rows, preferred_element_type=jnp.float32)
        part_sum = part_sum + jnp.dot(cycle_dense, cycle_rows, preferred_element_type=jnp.float32)
        return total + part_sum, None

    start_total = jnp.zeros((ROWS, COLS), jnp.float32)
    total, _ = lax.scan(add_group, start_total, jnp.arange(N_GRP, dtype=jnp.int32))
    ordered = total.reshape(ROW_TILES, TS, COLS)[owners].reshape(ROWS, COLS)
    return base + ordered
```

```python
import functools

import jax
import jax.numpy as jnp
from jax import lax
from jax.experimental import pallas as pl
from jax.experimental.pallas import tpu as pltpu
from jax.sharding import PartitionSpec as P

TS = 64
HALF = TS // 2
VMEM = pl.BlockSpec(memory_space=pltpu.VMEM)
SMEM = pl.BlockSpec(memory_space=pltpu.SMEM)


def ring_order(n):
    return list(range(0, n, 2)) + list(range(n - 1, 0, -2))


def rows_of(amps, count):
    tiles, slots, _ = amps.shape
    live = jnp.arange(slots, dtype=jnp.int32)[None, :] < count
    amps = jnp.where(live[:, :, None], amps, jnp.zeros_like(amps))
    return amps.reshape(tiles, slots * HALF, 2 * TS)


def all_ids(own, n_dev):
    table = own[None]
    step = 1
    while step < n_dev:
        swap = [(d, d ^ step) for d in range(n_dev)]
        table = jnp.concatenate([table, lax.ppermute(table, "dev", swap)], axis=0)
        step *= 2
    return table


def tile_kernel(n_tiles, ladder_slots, at_ref, core_ref, ids_ref, *refs):
    amp_refs = refs[:n_tiles]
    ladder_ref, cycle_ref, keep_ref, send_ref = refs[n_tiles:]
    slots = amp_refs[0].shape[0] // HALF
    cols = ladder_ref.shape[1]
    core = core_ref[0]
    for t in range(n_tiles):
        first = at_ref[t]
        total = jnp.zeros((TS, cols), jnp.float32)
        for q in range(0, slots, 4):
            left, right = [], []
            for s in range(q, min(q + 4, slots)):
                k = pl.multiple_of(ids_ref[first + s] * TS, TS)
                panel_ref = ladder_ref if s < ladder_slots else cycle_ref
                right.append(panel_ref[pl.ds(k, TS), :])
                tile = amp_refs[t][s * HALF : (s + 1) * HALF, :]
                left.append(jnp.concatenate([tile[:, :TS], tile[:, TS:]], axis=0))
            total += jnp.dot(
                jnp.concatenate(left, axis=1),
                jnp.concatenate(right, axis=0),
                preferred_element_type=jnp.float32,
            )
        rows = slice(t * TS, (t + 1) * TS)

        @pl.when(core == 0)
        def _():
            keep_ref[rows, :] = total[:, : cols // 2]
            send_ref[rows, :] = total[:, cols // 2 :]

        @pl.when(core != 0)
        def _():
            keep_ref[rows, :] = total[:, cols // 2 :]
            send_ref[rows, :] = total[:, : cols // 2]


def tile_products(amps, at, core, ids, ladder_panel, cycle_panel, ladder_slots):
    n, cols = len(amps), ladder_panel.shape[1]
    half = jax.ShapeDtypeStruct((n * TS, cols // 2), jnp.float32)
    slots = amps[0].shape[0] // HALF
    return pl.pallas_call(
        functools.partial(tile_kernel, n, ladder_slots),
        out_shape=(half, half),
        in_specs=[SMEM, SMEM, SMEM] + [VMEM] * (n + 2),
        out_specs=(VMEM, VMEM),
        compiler_params=pltpu.CompilerParams(vmem_limit_bytes=24 << 20),
        cost_estimate=pl.CostEstimate(
            flops=2 * n * TS * slots * TS * cols, bytes_accessed=4 << 20, transcendentals=0
        ),
    )(at, core, ids, *amps, ladder_panel, cycle_panel)


def pick_kernel(n_early, slot_ref, early_ref, own_ref, other_ref, mine_ref, partner_ref):
    owned = mine_ref.shape[0] // TS
    for i in range(2 * owned):
        slot = slot_ref[i]
        old = pl.multiple_of(jnp.minimum(slot, n_early - 1) * TS, TS)
        new = pl.multiple_of(jnp.maximum(slot - n_early, 0) * TS, TS)
        late = own_ref[pl.ds(new, TS), :]
        for ref in other_ref:
            late = late + ref[pl.ds(new, TS), :]
        value = jnp.where(slot < n_early, early_ref[pl.ds(old, TS), :], late)
        out_ref, at = (mine_ref, i) if i < owned else (partner_ref, i - owned)
        out_ref[at * TS : (at + 1) * TS, :] = value


def finish_kernel(core_ref, mine_ref, got_ref, base_ref, out_ref, rows_ref):
    rows, cols = base_ref.shape[0], base_ref.shape[1] // 2
    core = core_ref[0]
    for c in range(cols // 128):
        lane = slice(c * 128, (c + 1) * 128)
        for tile in range(rows // TS):
            for part in range(2):
                take = slice(tile * TS + part * HALF, tile * TS + (part + 1) * HALF)
                put = pl.ds(tile * TS + part, HALF, stride=2)
                mine, got = mine_ref[take, lane], got_ref[take, lane]
                rows_ref[0, put, :] = jnp.where(core == 0, mine, got)
                rows_ref[1, put, :] = jnp.where(core == 0, got, mine)
        for side in range(2):
            lane = slice(side * cols + c * 128, side * cols + (c + 1) * 128)
            out_ref[:, lane] = base_ref[:, lane] + rows_ref[side]


def per_device(
    ladder_amps,
    ladder_ids,
    ladder_count,
    cycle_amps,
    cycle_ids,
    cycle_count,
    ladder_panel,
    cycle_panel,
    owners,
    base,
):
    n_dev, n_grp = lax.axis_size("dev"), lax.axis_size("grp")
    me, grp = lax.axis_index("dev"), lax.axis_index("grp")
    core = (grp % 2).reshape(1)
    tiles, ladder_slots, _ = ladder_amps.shape
    slots = ladder_slots + cycle_amps.shape[1]
    order = ring_order(n_dev)
    place = [order.index(d) for d in range(n_dev)]
    forward = [(order[i], order[(i + 1) % n_dev]) for i in range(n_dev)]
    backward = [(b, a) for a, b in forward]
    swap = [(g, g ^ 1) for g in range(n_grp)]
    order_of, place_of = jnp.array(order, jnp.int32), jnp.array(place, jnp.int32)

    own = jnp.concatenate(
        [rows_of(ladder_amps, ladder_count), rows_of(cycle_amps, cycle_count)], axis=1
    )
    own = [own[t] for t in range(tiles)]
    ids = all_ids(jnp.concatenate([ladder_ids, cycle_ids], axis=1), n_dev).reshape(-1)

    def source(back):
        return order_of[(place_of[me] - back + n_dev) % n_dev]

    batches = [[(own[t], 0, t) for t in range(tiles)]]
    ahead, behind = own, own
    for step in range(1, n_dev // 2):
        ahead = [lax.ppermute(a, "dev", forward) for a in ahead]
        behind = [lax.ppermute(b, "dev", backward) for b in behind]
        batches.append(
            [(a, step, t) for t, a in enumerate(ahead)]
            + [(b, -step, t) for t, b in enumerate(behind)]
        )
    cut = tiles // 2
    batches.append(
        [(lax.ppermute(ahead[t], "dev", forward), n_dev // 2, t) for t in range(cut)]
        + [(lax.ppermute(behind[t], "dev", backward), n_dev // 2, t) for t in range(cut, tiles)]
    )

    where, early = [], []
    for number, batch in enumerate(batches):
        at = jnp.stack([(jnp.bitwise_xor(source(b), me) * tiles + t) * slots for _, b, t in batch])
        where += [source(b) * tiles + t for _, b, t in batch]
        keep, send = tile_products(
            [a for a, _, _ in batch], at, core, ids, ladder_panel, cycle_panel, ladder_slots
        )
        mine = keep + lax.ppermute(send, "grp", swap)
        others = [
            lax.ppermute(mine, "grp", [(g, (g + k) % n_grp) for g in range(n_grp)])
            for k in range(2, n_grp, 2)
        ]
        if number < len(batches) - 1:
            early.append(functools.reduce(jnp.add, others, mine))
    early = jnp.concatenate(early, axis=0)
    n_early = early.shape[0] // TS

    owned = owners.shape[0] // n_grp
    slot_of = jnp.argmax(owners[:, None] == jnp.stack(where)[None, :], axis=1).astype(jnp.int32)
    picks = jnp.concatenate(
        [
            lax.dynamic_slice_in_dim(slot_of, grp * owned, owned),
            lax.dynamic_slice_in_dim(slot_of, jnp.bitwise_xor(grp, 1) * owned, owned),
        ]
    )
    rows, cols = base.shape
    half = jax.ShapeDtypeStruct((rows, cols // 2), jnp.float32)
    picked, given = pl.pallas_call(
        lambda slot, old, new, *rest: pick_kernel(n_early, slot, old, new, rest[:-2], *rest[-2:]),
        out_shape=(half, half),
        in_specs=[SMEM] + [VMEM] * (2 + len(others)),
        out_specs=(VMEM, VMEM),
        compiler_params=pltpu.CompilerParams(vmem_limit_bytes=32 << 20),
    )(picks, early, mine, *others)
    got = lax.ppermute(given, "grp", swap)
    return pl.pallas_call(
        finish_kernel,
        out_shape=jax.ShapeDtypeStruct(base.shape, jnp.float32),
        in_specs=[SMEM, VMEM, VMEM, VMEM],
        out_specs=VMEM,
        scratch_shapes=[pltpu.VMEM((2, rows, 128), jnp.float32)],
        compiler_params=pltpu.CompilerParams(vmem_limit_bytes=16 << 20),
    )(core, picked, got, base)


def solution(mesh):
    placed = (
        P("dev", "grp", None),
        P("dev", "grp"),
        P("dev", "grp"),
        P("dev", "grp", None),
        P("dev", "grp"),
        P("dev", "grp"),
        P("grp", "dev"),
        P("grp", "dev"),
        P(),
        P("grp", "dev"),
    )
    return jax.shard_map(
        per_device, mesh=mesh, in_specs=placed, out_specs=P("grp", "dev"), check_vma=False
    )
```

```python
import functools

import jax
import jax.numpy as jnp
from jax import lax
from jax.experimental import pallas as pl
from jax.experimental.pallas import tpu as pltpu
from jax.sharding import PartitionSpec as P

TS = 64
HALF = TS // 2
LANES = 128
SCALE = 16.0
DEAD = 128
VMEM = pl.BlockSpec(memory_space=pltpu.VMEM)
SMEM = pl.BlockSpec(memory_space=pltpu.SMEM)


def ring_order(n):
    return list(range(0, n, 2)) + list(range(n - 1, 0, -2))


def ring_place(d, n):
    return jnp.where(lax.rem(d, 2) == 0, lax.div(d, 2), n - 1 - lax.div(d, 2))


def rows_of(amps):
    tiles, slots, _ = amps.shape
    return amps.reshape(tiles, slots * HALF, 2 * TS)


def marked(ids, count):
    slot = jnp.arange(ids.shape[1], dtype=jnp.int32)[None, :]
    return jnp.where(slot < count, ids, ids + DEAD)


def tile_kernel(n_tiles, ladder_slots, slots, ids_ref, *refs):
    amp_refs = refs[:n_tiles]
    ladder_ref, cycle_ref, out_ref = refs[n_tiles:]
    cols = ladder_ref.shape[1]
    for t in range(n_tiles):
        total = jnp.zeros((TS, cols), jnp.float32)
        for q in range(0, slots, 4):
            left, right = [], []
            for s in range(q, min(q + 4, slots)):
                mark = ids_ref[t * slots + s]
                k = pl.multiple_of(lax.rem(mark, DEAD) * TS, TS)
                panel_ref = ladder_ref if s < ladder_slots else cycle_ref
                right.append(panel_ref[pl.ds(k, TS), :])
                tile = amp_refs[t][s * HALF : (s + 1) * HALF, :]
                tile = jnp.where(mark < DEAD, tile, jnp.zeros_like(tile))
                left.append(jnp.concatenate([tile[:, :TS], tile[:, TS:]], axis=0))
            total += jnp.dot(
                jnp.concatenate(left, axis=1),
                jnp.concatenate(right, axis=0),
                preferred_element_type=jnp.float32,
            )
        for part in range(2):
            for c in range(cols // LANES):
                out_ref[t, c, pl.ds(part, HALF, stride=2), :] = total[
                    part * HALF : (part + 1) * HALF, c * LANES : (c + 1) * LANES
                ]


def tile_products(amps, ids, ladder_panel, cycle_panel, ladder_slots, slots):
    n, cols = len(amps), ladder_panel.shape[1]
    return pl.pallas_call(
        functools.partial(tile_kernel, n, ladder_slots, slots),
        out_shape=jax.ShapeDtypeStruct((n, cols // LANES, TS, LANES), jnp.float32),
        in_specs=[SMEM] + [VMEM] * (n + 2),
        out_specs=VMEM,
        compiler_params=pltpu.CompilerParams(vmem_limit_bytes=10 << 20),
        cost_estimate=pl.CostEstimate(flops=1, bytes_accessed=1, transcendentals=0),
    )(ids, *amps, ladder_panel, cycle_panel)


def arrival(row_tile, place, tiles, n_dev):
    t = lax.rem(row_tile, tiles)
    back = lax.rem(place - ring_place(lax.div(row_tile, tiles), n_dev) + n_dev, n_dev)
    half = n_dev // 2
    ahead = tiles + (back - 1) * 2 * tiles + t
    behind = tiles + (n_dev - back - 1) * 2 * tiles + tiles + t
    last = tiles + (half - 1) * 2 * tiles + t
    slot = jnp.where(back < half, ahead, jnp.where(back > half, behind, last))
    return jnp.where(back == 0, t, slot)


def pick_kernel(tiles, n_dev, n_grp, shifts, n_parts, me_ref, owners_ref, *refs):
    part_refs, out_refs = refs[:n_parts], refs[n_parts:]
    grp, place = me_ref[0], ring_place(me_ref[1], n_dev)
    for shift, out_ref in zip(shifts, out_refs):
        owner = lax.rem(grp + (shift if shift >= 0 else ~shift), n_grp)
        if shift < 0:
            owner = owner + 1 - 2 * lax.rem(owner, 2)
        owned = out_ref.shape[0]
        for i in range(owned):
            slot = arrival(owners_ref[owner * owned + i], place, tiles, n_dev)
            low = 0
            for part_ref in part_refs:
                high = low + part_ref.shape[0]

                @pl.when((slot >= low) & (slot < high))
                def _():
                    out_ref[i] = part_ref[jnp.clip(slot - low, 0, high - low - 1)]

                low = high


def finish_kernel(base_ref, *refs):
    sum_refs, out_ref = refs[:-1], refs[-1]
    for i in range(sum_refs[0].shape[0]):
        for c in range(sum_refs[0].shape[1]):
            at = (slice(i * TS, (i + 1) * TS), slice(c * LANES, (c + 1) * LANES))
            total = sum_refs[0][i, c]
            for ref in sum_refs[1:]:
                total = total + ref[i, c]
            out_ref[at] = base_ref[at] + total


def per_device(
    ladder_amps,
    ladder_ids,
    ladder_count,
    cycle_amps,
    cycle_ids,
    cycle_count,
    ladder_panel,
    cycle_panel,
    owners,
    base,
):
    n_dev, n_grp = lax.axis_size("dev"), lax.axis_size("grp")
    me = jnp.stack([lax.axis_index("grp"), lax.axis_index("dev")])
    tiles, ladder_slots, _ = ladder_amps.shape
    slots = ladder_slots + cycle_amps.shape[1]
    order = ring_order(n_dev)
    forward = [(order[i], order[(i + 1) % n_dev]) for i in range(n_dev)]
    backward = [(b, a) for a, b in forward]
    swap = [(g, g ^ 1) for g in range(n_grp)]

    own = jnp.concatenate([rows_of(ladder_amps), rows_of(cycle_amps)], axis=1)
    marks = jnp.concatenate(
        [marked(ladder_ids, ladder_count), marked(cycle_ids, cycle_count)], axis=1
    ).reshape(1, -1)
    note = jnp.pad(marks.astype(jnp.bfloat16), ((0, 7), (0, 2 * TS - marks.size)))
    own = [jnp.concatenate([own[0], note], axis=0)] + [own[t] for t in range(1, tiles)]

    def marks_of(piece):
        return piece[slots * HALF, : tiles * slots].astype(jnp.int32)

    def products(amps, ids):
        return tile_products(amps, ids, ladder_panel, cycle_panel, ladder_slots, slots)

    cut = tiles // 2
    waves = [(range(cut), range(cut, tiles)), (range(cut, tiles), range(cut))]

    def hop(wave, pieces):
        ahead, behind = waves[wave]
        return {
            **{(0, t): lax.ppermute(pieces[0, t], "dev", forward) for t in ahead},
            **{(1, t): lax.ppermute(pieces[1, t], "dev", backward) for t in behind},
        }

    def landed_products(batches):
        amps = [piece for pieces, _ in batches for piece in pieces]
        return products(amps, jnp.concatenate([marks for _, marks in batches]))

    def batch(landed):
        pieces = [landed[side, t] for side in range(2) for t in range(tiles)]
        return pieces, jnp.concatenate([marks_of(landed[side, 0]) for side in range(2)])

    batches = [(own, marks.reshape(-1))]
    start = {(side, t): own[t] for side in range(2) for t in range(tiles)}
    flying = [hop(wave, start) for wave in range(2)]
    for _ in range(1, n_dev // 2 - 1):
        batches.append(batch({**flying[0], **flying[1]}))
        flying = [hop(wave, flying[wave]) for wave in range(2)]
    first, batches = lax.optimization_barrier((flying[0], batches))
    last = hop(0, first)
    parts = [landed_products(batches[i : i + 3]) for i in range(0, len(batches), 3)]
    second, parts = lax.optimization_barrier((flying[1], parts))
    parts.append(landed_products([batch({**first, **second})]))
    amps = [last[0 if t < cut else 1, t] for t in range(tiles)]
    parts.append(products(amps, marks_of(amps[0])))

    rows, cols = base.shape
    owned = jax.ShapeDtypeStruct((rows // TS, cols // LANES, TS, LANES), jnp.float32)

    def pick(*shifts):
        return pl.pallas_call(
            functools.partial(pick_kernel, tiles, n_dev, n_grp, shifts, len(parts)),
            out_shape=(owned,) * len(shifts),
            in_specs=[SMEM, SMEM] + [VMEM] * len(parts),
            out_specs=(VMEM,) * len(shifts),
            compiler_params=pltpu.CompilerParams(vmem_limit_bytes=10 << 20),
            cost_estimate=pl.CostEstimate(flops=1, bytes_accessed=1, transcendentals=0),
        )(me, owners, *parts)

    others = []
    for shift in range(2, n_grp, 2):
        mine, partners = pick(shift, ~shift)
        chip = mine + lax.ppermute(partners, "grp", swap)
        sent = lax.ppermute(
            (chip * SCALE).astype(jnp.float16), "grp", [(g, (g + shift) % n_grp) for g in range(n_grp)]
        )
        others.append(sent.astype(jnp.float32) * (1 / SCALE))
    mine, partners = pick(0, ~0)
    chip = mine + lax.ppermute(partners, "grp", swap)
    return pl.pallas_call(
        finish_kernel,
        out_shape=jax.ShapeDtypeStruct(base.shape, jnp.float32),
        in_specs=[VMEM] * (2 + len(others)),
        out_specs=VMEM,
        compiler_params=pltpu.CompilerParams(vmem_limit_bytes=10 << 20),
    )(base, chip, *others)


def solution(mesh):
    placed = (
        P("dev", "grp", None),
        P("dev", "grp"),
        P("dev", "grp"),
        P("dev", "grp", None),
        P("dev", "grp"),
        P("dev", "grp"),
        P("grp", "dev"),
        P("grp", "dev"),
        P(),
        P("grp", "dev"),
    )
    return jax.shard_map(
        per_device, mesh=mesh, in_specs=placed, out_specs=P("grp", "dev"), check_vma=False
    )
```

```python
import functools

import jax
import jax.numpy as jnp
from jax import lax
from jax.experimental import pallas as pl
from jax.experimental.pallas import tpu as pltpu
from jax.sharding import PartitionSpec as P

TS = 64
HALF = TS // 2
LANES = 128
SCALE = 16.0
DEAD = 128
VMEM = pl.BlockSpec(memory_space=pltpu.VMEM)
SMEM = pl.BlockSpec(memory_space=pltpu.SMEM)


def ring_order(n):
    return list(range(0, n, 2)) + list(range(n - 1, 0, -2))


def ring_place(d, n):
    return jnp.where(lax.rem(d, 2) == 0, lax.div(d, 2), n - 1 - lax.div(d, 2))


def rows_of(amps):
    tiles, slots, _ = amps.shape
    return amps.reshape(tiles, slots * HALF, 2 * TS)


def marked(ids, count):
    slot = jnp.arange(ids.shape[1], dtype=jnp.int32)[None, :]
    return jnp.where(slot < count, ids, ids + DEAD)


def multiply(ids_ref, amp_refs, ladder_ref, cycle_ref, ladder_slots, slots, rows_ref, out_ref):
    cols = ladder_ref.shape[1]
    for t, amp_ref in enumerate(amp_refs):
        total = jnp.zeros((TS, cols), jnp.float32)
        for q in range(0, slots, 4):
            left, right = [], []
            for s in range(q, min(q + 4, slots)):
                mark = ids_ref[t * slots + s]
                k = pl.multiple_of(lax.rem(mark, DEAD) * TS, TS)
                panel_ref = ladder_ref if s < ladder_slots else cycle_ref
                right.append(panel_ref[pl.ds(k, TS), :])
                tile = amp_ref[s * HALF : (s + 1) * HALF, :]
                tile = jnp.where(mark < DEAD, tile, jnp.zeros_like(tile))
                left.append(jnp.concatenate([tile[:, :TS], tile[:, TS:]], axis=0))
            total += jnp.dot(
                jnp.concatenate(left, axis=1),
                jnp.concatenate(right, axis=0),
                preferred_element_type=jnp.float32,
            )
        for c in range(cols // LANES):
            lanes = slice(c * LANES, (c + 1) * LANES)
            for part in range(2):
                rows_ref[t % 2, c, pl.ds(part, HALF, stride=2), :] = total[
                    part * HALF : (part + 1) * HALF, lanes
                ]
            out_ref[t * TS : (t + 1) * TS, lanes] = rows_ref[t % 2, c]


def pick(slot_ref, first, part_refs, out_ref):
    for i in range(out_ref.shape[0] // TS):
        slot = slot_ref[first + i]
        low = 0
        for part_ref in part_refs:
            high = low + part_ref.shape[0] // TS

            @pl.when((slot >= low) & (slot < high))
            def _():
                at = pl.multiple_of(jnp.clip(slot - low, 0, high - low - 1) * TS, TS)
                out_ref[i * TS : (i + 1) * TS, :] = part_ref[pl.ds(at, TS), :]

            low = high


def tile_kernel(n, ladder_slots, slots, ids_ref, *refs):
    ladder_ref, cycle_ref, out_ref, rows_ref = refs[n:]
    multiply(ids_ref, refs[:n], ladder_ref, cycle_ref, ladder_slots, slots, rows_ref, out_ref)


def last_kernel(n, ladder_slots, slots, n_parts, ids_ref, slot_ref, *refs):
    amp_refs, (ladder_ref, cycle_ref), part_refs = refs[:n], refs[n : n + 2], refs[n + 2 :][:n_parts]
    late_ref, *out_refs, rows_ref = refs[n + 2 + n_parts :]
    multiply(ids_ref, amp_refs, ladder_ref, cycle_ref, ladder_slots, slots, rows_ref, late_ref)
    first = 0
    for out_ref in out_refs:
        pick(slot_ref, first, part_refs + (late_ref,), out_ref)
        first += out_ref.shape[0] // TS


def own_kernel(first, n_parts, slot_ref, *refs):
    for out_ref in refs[n_parts:]:
        pick(slot_ref, first, refs[:n_parts], out_ref)
        first += out_ref.shape[0] // TS


def call(kernel, out_shape, n_smem, args, scratch=()):
    return pl.pallas_call(
        kernel,
        out_shape=out_shape,
        in_specs=[SMEM] * n_smem + [VMEM] * (len(args) - n_smem),
        out_specs=jax.tree.map(lambda _: VMEM, out_shape),
        scratch_shapes=list(scratch),
        compiler_params=pltpu.CompilerParams(vmem_limit_bytes=12 << 20),
        cost_estimate=pl.CostEstimate(flops=1, bytes_accessed=1, transcendentals=0),
    )(*args)


def arrival(row_tile, place, tiles, n_dev):
    t = lax.rem(row_tile, tiles)
    back = lax.rem(place - ring_place(lax.div(row_tile, tiles), n_dev) + n_dev, n_dev)
    half = n_dev // 2
    ahead = tiles + (back - 1) * 2 * tiles + t
    behind = tiles + (n_dev - back - 1) * 2 * tiles + tiles + t
    last = tiles + (half - 1) * 2 * tiles + t
    slot = jnp.where(back < half, ahead, jnp.where(back > half, behind, last))
    return jnp.where(back == 0, t, slot)


def per_device(
    ladder_amps,
    ladder_ids,
    ladder_count,
    cycle_amps,
    cycle_ids,
    cycle_count,
    ladder_panel,
    cycle_panel,
    owners,
    base,
):
    n_dev, n_grp = lax.axis_size("dev"), lax.axis_size("grp")
    tiles, ladder_slots, _ = ladder_amps.shape
    slots = ladder_slots + cycle_amps.shape[1]
    order = ring_order(n_dev)
    forward = [(order[i], order[(i + 1) % n_dev]) for i in range(n_dev)]
    backward = [(b, a) for a, b in forward]
    swap = [(g, g ^ 1) for g in range(n_grp)]

    own = jnp.concatenate([rows_of(ladder_amps), rows_of(cycle_amps)], axis=1)
    marks = jnp.concatenate(
        [marked(ladder_ids, ladder_count), marked(cycle_ids, cycle_count)], axis=1
    ).reshape(1, -1)
    note = jnp.pad(marks.astype(jnp.bfloat16), ((0, 7), (0, 2 * TS - marks.size)))
    own = [jnp.concatenate([own[0], note], axis=0)] + [own[t] for t in range(1, tiles)]

    def marks_of(piece):
        return piece[slots * HALF, : tiles * slots].astype(jnp.int32)

    cols = base.shape[1]
    rows_scratch = [pltpu.VMEM((2, cols // LANES, TS, LANES), jnp.float32)]

    def products(amps, ids):
        return call(
            functools.partial(tile_kernel, len(amps), ladder_slots, slots),
            jax.ShapeDtypeStruct((len(amps) * TS, cols), jnp.float32),
            1,
            [ids, *amps, ladder_panel, cycle_panel],
            rows_scratch,
        )

    grp, place = lax.axis_index("grp"), ring_place(lax.axis_index("dev"), n_dev)
    owned = owners.shape[0] // n_grp
    slot_of = arrival(owners, place, tiles, n_dev).reshape(n_grp, owned)
    shifts = [*range(2, n_grp, 2), 0]
    ahead = (grp + jnp.array(shifts, jnp.int32)) % n_grp
    chosen = jnp.stack([ahead, ahead ^ 1], axis=1).reshape(-1, 1)
    picked = chosen == jnp.arange(n_grp, dtype=jnp.int32)[None, :]
    slot_of = jnp.sum(jnp.where(picked[:, :, None], slot_of[None], 0), axis=1).reshape(-1)

    cut = tiles // 2
    waves = [(range(cut), range(cut, tiles)), (range(cut, tiles), range(cut))]

    def hop(wave, pieces):
        ahead, behind = waves[wave]
        return {
            **{(0, t): lax.ppermute(pieces[0, t], "dev", forward) for t in ahead},
            **{(1, t): lax.ppermute(pieces[1, t], "dev", backward) for t in behind},
        }

    def batch(landed):
        pieces = [landed[side, t] for side in range(2) for t in range(tiles)]
        return pieces, jnp.concatenate([marks_of(landed[side, 0]) for side in range(2)])

    start = {(side, t): own[t] for side in range(2) for t in range(tiles)}
    flying = [hop(wave, start) for wave in range(2)]
    parts = [products(own, marks.reshape(-1))]
    for _ in range(1, n_dev // 2 - 1):
        first, parts = lax.optimization_barrier((flying[0], parts))
        landed = batch({**first, **flying[1]})
        flying = [hop(0, first), hop(1, flying[1])]
        parts.append(products(*landed))
    first, parts = lax.optimization_barrier((flying[0], parts))
    last = hop(0, first)
    parts.append(products(*batch({**first, **flying[1]})))
    amps = [last[0 if t < cut else 1, t] for t in range(tiles)]
    tile_rows = jax.ShapeDtypeStruct((owned * TS, cols), jnp.float32)
    late, *rows_for = call(
        functools.partial(last_kernel, len(amps), ladder_slots, slots, len(parts)),
        (jax.ShapeDtypeStruct((len(amps) * TS, cols), jnp.float32),) + (tile_rows,) * (n_grp - 2),
        2,
        [marks_of(amps[0]), slot_of, *amps, ladder_panel, cycle_panel, *parts],
        rows_scratch,
    )
    total = base
    for k, shift in enumerate(shifts[:-1]):
        chip = rows_for[2 * k] + lax.ppermute(rows_for[2 * k + 1], "grp", swap)
        sent = lax.ppermute(
            (chip * SCALE).astype(jnp.float16), "grp", [(g, (g + shift) % n_grp) for g in range(n_grp)]
        )
        total = total + sent.astype(jnp.float32) * (1 / SCALE)
    mine, partners = call(
        functools.partial(own_kernel, (n_grp - 2) * owned, len(parts) + 1),
        (tile_rows, tile_rows),
        1,
        [slot_of, *parts, late],
    )
    return total + (mine + lax.ppermute(partners, "grp", swap))


def solution(mesh):
    placed = (
        P("dev", "grp", None),
        P("dev", "grp"),
        P("dev", "grp"),
        P("dev", "grp", None),
        P("dev", "grp"),
        P("dev", "grp"),
        P("grp", "dev"),
        P("grp", "dev"),
        P(),
        P("grp", "dev"),
    )
    return jax.shard_map(
        per_device, mesh=mesh, in_specs=placed, out_specs=P("grp", "dev"), check_vma=False
    )
```

```python
import functools
import math

import jax
import jax.numpy as jnp
from jax import lax
from jax.experimental import pallas as pl
from jax.experimental.pallas import tpu as pltpu
from jax.sharding import PartitionSpec as P

TS = 64
HALF = TS // 2
LANES = 128
SCALE = 16.0
DEAD = 128
MARGIN = 1
VMEM = pl.BlockSpec(memory_space=pltpu.VMEM)
SMEM = pl.BlockSpec(memory_space=pltpu.SMEM)


def ring_order(n):
    return list(range(0, n, 2)) + list(range(n - 1, 0, -2))


def ring_place(d, n):
    return jnp.where(lax.rem(d, 2) == 0, lax.div(d, 2), n - 1 - lax.div(d, 2))


def rows_of(amps):
    tiles, slots, _ = amps.shape
    return amps.reshape(tiles, slots * HALF, 2 * TS)


def marked(ids, count):
    slot = jnp.arange(ids.shape[1], dtype=jnp.int32)[None, :]
    return jnp.where(slot < count, ids, ids + DEAD)


def multiply(ids_ref, amp_refs, ladder_ref, cycle_ref, ladder_slots, slots, rows_ref, out_ref):
    cols = ladder_ref.shape[1]
    for t, amp_ref in enumerate(amp_refs):
        total = jnp.zeros((TS, cols), jnp.float32)
        for q in range(0, slots, 4):
            left, right = [], []
            for s in range(q, min(q + 4, slots)):
                mark = ids_ref[t * slots + s]
                k = pl.multiple_of(lax.rem(mark, DEAD) * TS, TS)
                panel_ref = ladder_ref if s < ladder_slots else cycle_ref
                right.append(panel_ref[pl.ds(k, TS), :])
                tile = amp_ref[s * HALF : (s + 1) * HALF, :]
                tile = jnp.where(mark < DEAD, tile, jnp.zeros_like(tile))
                left.append(jnp.concatenate([tile[:, :TS], tile[:, TS:]], axis=0))
            total += jnp.dot(
                jnp.concatenate(left, axis=1),
                jnp.concatenate(right, axis=0),
                preferred_element_type=jnp.float32,
            )
        for c in range(cols // LANES):
            lanes = slice(c * LANES, (c + 1) * LANES)
            for part in range(2):
                rows_ref[t % 2, c, pl.ds(part, HALF, stride=2), :] = total[
                    part * HALF : (part + 1) * HALF, lanes
                ]
            out_ref[t * TS : (t + 1) * TS, lanes] = rows_ref[t % 2, c]


def arrival(row_tile, place, tiles, n_dev):
    t = lax.rem(row_tile, tiles)
    back = lax.rem(place - ring_place(lax.div(row_tile, tiles), n_dev) + n_dev, n_dev)
    half, cut = n_dev // 2, tiles // 2
    step = jnp.minimum(back, n_dev - back)
    there = jnp.where(back < half, jnp.where(t < cut, t, t + cut), jnp.where(t < cut, t + tiles + cut, t))
    slot = tiles + (step - 1) * 2 * tiles + jnp.where(back == half, t, there)
    return jnp.where(back == 0, t, slot)


def slots_of(group, owned, tiles, n_dev, me_ref, owners_ref):
    place = ring_place(me_ref[1], n_dev)
    return [arrival(owners_ref[group * owned + i], place, tiles, n_dev) for i in range(owned)]


def tile_rows(ref, at):
    return ref.at[pl.ds(pl.multiple_of(at * TS, TS), TS), :]


def pick(part_refs, slots, out_ref):
    for i, slot in enumerate(slots):
        low = 0
        for part_ref in part_refs:
            high = low + part_ref.shape[0] // TS

            @pl.when((slot >= low) & (slot < high))
            def _():
                at = jnp.clip(slot - low, 0, high - low - 1)
                out_ref[i * TS : (i + 1) * TS, :] = tile_rows(part_ref, at)[...]

            low = high


def partner(group):
    return group + 1 - 2 * lax.rem(group, 2)


def tile_kernel(n, ladder_slots, slots, ids_ref, *refs):
    ladder_ref, cycle_ref, out_ref, rows_ref = refs[n:]
    multiply(ids_ref, refs[:n], ladder_ref, cycle_ref, ladder_slots, slots, rows_ref, out_ref)


def last_kernel(n, ladder_slots, slots, n_parts, tiles, n_dev, n_grp, ids_ref, me_ref, owners_ref, *refs):
    amp_refs, (ladder_ref, cycle_ref), part_refs = refs[:n], refs[n : n + 2], refs[n + 2 :][:n_parts]
    new_ref, *out_refs, rows_ref = refs[n + 2 + n_parts :]
    multiply(ids_ref, amp_refs, ladder_ref, cycle_ref, ladder_slots, slots, rows_ref, new_ref)
    owned = out_refs[0].shape[0] // TS
    for k, shift in enumerate(range(2, n_grp, 2)):
        group = lax.rem(me_ref[0] + shift, n_grp)
        for owner, out_ref in zip((group, partner(group)), out_refs[2 * k :]):
            pick(part_refs + (new_ref,), slots_of(owner, owned, tiles, n_dev, me_ref, owners_ref), out_ref)


def own_kernel(n_parts, tiles, n_dev, me_ref, owners_ref, *refs):
    owned = refs[-1].shape[0] // TS
    for owner, out_ref in zip((me_ref[0], partner(me_ref[0])), refs[n_parts:]):
        pick(refs[:n_parts], slots_of(owner, owned, tiles, n_dev, me_ref, owners_ref), out_ref)


def call(kernel, out_shape, n_smem, args, scratch=()):
    held = [*args, *jax.tree.leaves(out_shape)]
    held = sum(math.prod(x.shape) * x.dtype.itemsize for x in held)
    return pl.pallas_call(
        kernel,
        out_shape=out_shape,
        in_specs=[SMEM] * n_smem + [VMEM] * (len(args) - n_smem),
        out_specs=jax.tree.map(lambda _: VMEM, out_shape),
        scratch_shapes=list(scratch),
        compiler_params=pltpu.CompilerParams(vmem_limit_bytes=held + (MARGIN << 20)),
        cost_estimate=pl.CostEstimate(flops=1, bytes_accessed=1, transcendentals=0),
    )(*args)


def per_device(
    ladder_amps,
    ladder_ids,
    ladder_count,
    cycle_amps,
    cycle_ids,
    cycle_count,
    ladder_panel,
    cycle_panel,
    owners,
    base,
):
    n_dev, n_grp = lax.axis_size("dev"), lax.axis_size("grp")
    tiles, ladder_slots, _ = ladder_amps.shape
    slots = ladder_slots + cycle_amps.shape[1]
    order = ring_order(n_dev)
    forward = [(order[i], order[(i + 1) % n_dev]) for i in range(n_dev)]
    backward = [(b, a) for a, b in forward]
    swap = [(g, g ^ 1) for g in range(n_grp)]

    own = jnp.concatenate([rows_of(ladder_amps), rows_of(cycle_amps)], axis=1)
    marks = jnp.concatenate(
        [marked(ladder_ids, ladder_count), marked(cycle_ids, cycle_count)], axis=1
    ).reshape(1, -1)
    note = jnp.pad(marks.astype(jnp.bfloat16), ((0, 7), (0, 2 * TS - marks.size)))
    own = [jnp.concatenate([own[t], note], axis=0) for t in range(tiles)]

    def marks_of(piece, t):
        return piece[slots * HALF, t * slots : (t + 1) * slots].astype(jnp.int32)

    cols = base.shape[1]
    rows_scratch = [pltpu.VMEM((2, cols // LANES, TS, LANES), jnp.float32)]

    def products(amps, ids):
        return call(
            functools.partial(tile_kernel, len(amps), ladder_slots, slots),
            jax.ShapeDtypeStruct((len(amps) * TS, cols), jnp.float32),
            1,
            [ids, *amps, ladder_panel, cycle_panel],
            rows_scratch,
        )

    me = jnp.stack([lax.axis_index("grp"), lax.axis_index("dev")])
    owned = owners.shape[0] // n_grp
    shifts = range(2, n_grp, 2)

    def sums(n):
        return jax.ShapeDtypeStruct((n * TS, cols), jnp.float32)

    cut = tiles // 2
    waves = [
        [(t < cut, t) for t in range(tiles)],
        [(t >= cut, t) for t in (*range(cut, tiles), *range(cut))],
    ]

    def hop(wave, pieces):
        return [
            lax.ppermute(piece, "dev", forward if ahead else backward)
            for (ahead, _), piece in zip(waves[wave], pieces)
        ]

    def marks_in(wave, pieces):
        return jnp.concatenate([marks_of(piece, t) for (_, t), piece in zip(waves[wave], pieces)])

    def products_of(wave, pieces):
        return products(pieces, marks_in(wave, pieces))

    first = hop(0, [own[t] for _, t in waves[0]])
    parts = [products(own, marks.reshape(-1))]
    own, parts = lax.optimization_barrier((own, parts))
    second = hop(1, [own[t] for _, t in waves[1]])
    for step in range(1, n_dev // 2):
        first, parts = lax.optimization_barrier((first, parts))
        landed, first = first, hop(0, first)
        if step < n_dev // 2 - 1:
            parts.append(products_of(0, landed))
            second, parts = lax.optimization_barrier((second, parts))
            landed, second = second, hop(1, second)
            parts.append(products_of(1, landed))
        else:
            parts.append(products_of(0, landed))
            second, parts = lax.optimization_barrier((second, parts))
    pieces = second + first
    new, *leaving = call(
        functools.partial(
            last_kernel, len(pieces), ladder_slots, slots, len(parts), tiles, n_dev, n_grp
        ),
        (sums(len(pieces)),) + (sums(owned),) * (n_grp - 2),
        3,
        [
            jnp.concatenate([marks_in(1, second), marks_in(0, first)]),
            me,
            owners,
            *pieces,
            ladder_panel,
            cycle_panel,
            *parts,
        ],
        rows_scratch,
    )
    parts.append(new)
    total = base
    for k, shift in enumerate(shifts):
        chip = leaving[2 * k] + lax.ppermute(leaving[2 * k + 1], "grp", swap)
        sent = lax.ppermute(
            (chip * SCALE).astype(jnp.float16), "grp", [(g, (g + shift) % n_grp) for g in range(n_grp)]
        )
        total = total + sent.astype(jnp.float32) * (1 / SCALE)
    mine, partners = call(
        functools.partial(own_kernel, len(parts), tiles, n_dev),
        (sums(owned), sums(owned)),
        2,
        [me, owners, *parts],
    )
    return total + (mine + lax.ppermute(partners, "grp", swap))


def solution(mesh):
    placed = (
        P("dev", "grp", None),
        P("dev", "grp"),
        P("dev", "grp"),
        P("dev", "grp", None),
        P("dev", "grp"),
        P("dev", "grp"),
        P("grp", "dev"),
        P("grp", "dev"),
        P(),
        P("grp", "dev"),
    )
    return jax.shard_map(
        per_device, mesh=mesh, in_specs=placed, out_specs=P("grp", "dev"), check_vma=False
    )
```

```python
import functools
import math

import jax
import jax.numpy as jnp
from jax import lax
from jax.experimental import pallas as pl
from jax.experimental.pallas import tpu as pltpu
from jax.sharding import PartitionSpec as P

TS = 64
HALF = TS // 2
LANES = 128
SCALE = 16.0
DEAD = 128
MARGIN = 1
VMEM = pl.BlockSpec(memory_space=pltpu.VMEM)
SMEM = pl.BlockSpec(memory_space=pltpu.SMEM)


def ring_order(n):
    return list(range(0, n, 2)) + list(range(n - 1, 0, -2))


def ring_place(d, n):
    return jnp.where(lax.rem(d, 2) == 0, lax.div(d, 2), n - 1 - lax.div(d, 2))


def rows_of(amps):
    tiles, slots, _ = amps.shape
    return amps.reshape(tiles, slots * HALF, 2 * TS)


def marked(ids, count):
    slot = jnp.arange(ids.shape[1], dtype=jnp.int32)[None, :]
    return jnp.where(slot < count, ids, ids + DEAD)


def multiply(ids_ref, amp_refs, ladder_ref, cycle_ref, ladder_slots, slots, rows_ref, out_ref):
    cols = ladder_ref.shape[1]
    for t, amp_ref in enumerate(amp_refs):
        total = jnp.zeros((TS, cols), jnp.float32)
        for q in range(0, slots, 4):
            left, right = [], []
            for s in range(q, min(q + 4, slots)):
                mark = ids_ref[t * slots + s]
                k = pl.multiple_of(lax.rem(mark, DEAD) * TS, TS)
                panel_ref = ladder_ref if s < ladder_slots else cycle_ref
                right.append(panel_ref[pl.ds(k, TS), :])
                tile = amp_ref[s * HALF : (s + 1) * HALF, :]
                tile = jnp.where(mark < DEAD, tile, jnp.zeros_like(tile))
                left.append(jnp.concatenate([tile[:, :TS], tile[:, TS:]], axis=0))
            total += jnp.dot(
                jnp.concatenate(left, axis=1),
                jnp.concatenate(right, axis=0),
                preferred_element_type=jnp.float32,
            )
        for c in range(cols // LANES):
            lanes = slice(c * LANES, (c + 1) * LANES)
            for part in range(2):
                rows_ref[t % 2, c, pl.ds(part, HALF, stride=2), :] = total[
                    part * HALF : (part + 1) * HALF, lanes
                ]
            out_ref[t * TS : (t + 1) * TS, lanes] = rows_ref[t % 2, c]


def arrival(row_tile, place, tiles, n_dev):
    t = lax.rem(row_tile, tiles)
    back = lax.rem(place - ring_place(lax.div(row_tile, tiles), n_dev) + n_dev, n_dev)
    half, cut = n_dev // 2, tiles // 2
    step = jnp.minimum(back, n_dev - back)
    there = jnp.where(back < half, jnp.where(t < cut, t, t + cut), jnp.where(t < cut, t + tiles + cut, t))
    slot = tiles + (step - 1) * 2 * tiles + jnp.where(back == half, t, there)
    return jnp.where(back == 0, t, slot)


def slots_of(group, owned, tiles, n_dev, me_ref, owners_ref):
    place = ring_place(me_ref[1], n_dev)
    slots = [arrival(owners_ref[group * owned + i], place, tiles, n_dev) for i in range(owned)]
    ranks = [sum((other < slot).astype(jnp.int32) for other in slots) for slot in slots]
    return list(zip(slots, ranks))


def tile_rows(ref, at):
    return ref.at[pl.ds(pl.multiple_of(at * TS, TS), TS), :]


def pick(part_refs, slot, out_ref, at, wanted=True):
    low = 0
    for part_ref in part_refs:
        high = low + part_ref.shape[0] // TS

        @pl.when((slot >= low) & (slot < high) & wanted)
        def _():
            tile_rows(out_ref, at)[...] = tile_rows(part_ref, jnp.clip(slot - low, 0, high - low - 1))[...]

        low = high


def partner(group):
    return group + 1 - 2 * lax.rem(group, 2)


def tile_kernel(n, ladder_slots, slots, ids_ref, *refs):
    ladder_ref, cycle_ref, out_ref, rows_ref = refs[n:]
    multiply(ids_ref, refs[:n], ladder_ref, cycle_ref, ladder_slots, slots, rows_ref, out_ref)


def leaving_kernel(
    n, ladder_slots, slots, n_parts, tiles, n_dev, n_grp, owned, ranks, ids_ref, me_ref, owners_ref, *refs
):
    amp_refs, (ladder_ref, cycle_ref), part_refs = refs[:n], refs[n : n + 2], refs[n + 2 :][:n_parts]
    new_ref, *out_refs, rows_ref = refs[n + 2 + n_parts :]
    multiply(ids_ref, amp_refs, ladder_ref, cycle_ref, ladder_slots, slots, rows_ref, new_ref)
    for k, shift in enumerate(range(2, n_grp, 2)):
        group = lax.rem(me_ref[0] + shift, n_grp)
        for owner, out_ref in zip((group, partner(group)), out_refs[2 * k :]):
            for slot, rank in slots_of(owner, owned, tiles, n_dev, me_ref, owners_ref):
                wanted = (rank >= ranks.start) & (rank < ranks.stop)
                at = jnp.clip(rank - ranks.start, 0, len(ranks) - 1)
                pick(part_refs + (new_ref,), slot, out_ref, at, wanted)


def staying_kernel(n_parts, tiles, n_dev, owned, me_ref, owners_ref, *refs):
    for owner, out_ref in zip((me_ref[0], partner(me_ref[0])), refs[n_parts:]):
        for i, (slot, _) in enumerate(slots_of(owner, owned, tiles, n_dev, me_ref, owners_ref)):
            pick(refs[:n_parts], slot, out_ref, i)


def finish_kernel(tiles, n_dev, owned, me_ref, owners_ref, base_ref, mine_ref, got_ref, *refs):
    other_refs, out_ref = refs[:-1], refs[-1]
    for i, (_, rank) in enumerate(slots_of(me_ref[0], owned, tiles, n_dev, me_ref, owners_ref)):
        rows = slice(i * TS, (i + 1) * TS)
        total = base_ref[rows, :] + (mine_ref[rows, :] + got_ref[rows, :])
        for soon_ref, late_ref in zip(other_refs[::2], other_refs[1::2]):
            n_soon = soon_ref.shape[0] // TS
            soon = tile_rows(soon_ref, jnp.minimum(rank, n_soon - 1))[...]
            late = tile_rows(late_ref, jnp.maximum(rank - n_soon, 0))[...]
            total = total + jnp.where(rank < n_soon, soon, late)
        out_ref[rows, :] = total


def call(kernel, out_shape, n_smem, args, scratch=()):
    held = [*args, *jax.tree.leaves(out_shape)]
    held = sum(math.prod(x.shape) * x.dtype.itemsize for x in held)
    return pl.pallas_call(
        kernel,
        out_shape=out_shape,
        in_specs=[SMEM] * n_smem + [VMEM] * (len(args) - n_smem),
        out_specs=jax.tree.map(lambda _: VMEM, out_shape),
        scratch_shapes=list(scratch),
        compiler_params=pltpu.CompilerParams(vmem_limit_bytes=held + (MARGIN << 20)),
        cost_estimate=pl.CostEstimate(flops=1, bytes_accessed=1, transcendentals=0),
    )(*args)


def per_device(
    ladder_amps,
    ladder_ids,
    ladder_count,
    cycle_amps,
    cycle_ids,
    cycle_count,
    ladder_panel,
    cycle_panel,
    owners,
    base,
):
    n_dev, n_grp = lax.axis_size("dev"), lax.axis_size("grp")
    tiles, ladder_slots, _ = ladder_amps.shape
    slots = ladder_slots + cycle_amps.shape[1]
    order = ring_order(n_dev)
    forward = [(order[i], order[(i + 1) % n_dev]) for i in range(n_dev)]
    backward = [(b, a) for a, b in forward]
    swap = [(g, g ^ 1) for g in range(n_grp)]

    own = rows_of(jnp.concatenate([ladder_amps, cycle_amps], axis=1))
    own, ladder_ids, ladder_count, cycle_ids, cycle_count = lax.optimization_barrier(
        (own, ladder_ids, ladder_count, cycle_ids, cycle_count)
    )
    marks = jnp.concatenate(
        [marked(ladder_ids, ladder_count), marked(cycle_ids, cycle_count)], axis=1
    ).reshape(1, -1)
    note = jnp.pad(marks.astype(jnp.bfloat16), ((0, 7), (0, 2 * TS - marks.size)))
    own = [jnp.concatenate([own[t], note], axis=0) for t in range(tiles)]

    def marks_of(piece, t):
        return piece[slots * HALF, t * slots : (t + 1) * slots].astype(jnp.int32)

    cols = base.shape[1]
    rows_scratch = [pltpu.VMEM((2, cols // LANES, TS, LANES), jnp.float32)]

    def products(amps, ids):
        return call(
            functools.partial(tile_kernel, len(amps), ladder_slots, slots),
            jax.ShapeDtypeStruct((len(amps) * TS, cols), jnp.float32),
            1,
            [ids, *amps, ladder_panel, cycle_panel],
            rows_scratch,
        )

    me = jnp.stack([lax.axis_index("grp"), lax.axis_index("dev")])
    owned = owners.shape[0] // n_grp
    shifts = range(2, n_grp, 2)

    def sums(n):
        return jax.ShapeDtypeStruct((n * TS, cols), jnp.float32)

    cut = tiles // 2
    waves = [
        [(t < cut, t) for t in range(tiles)],
        [(t >= cut, t) for t in (*range(cut, tiles), *range(cut))],
    ]

    def hop(wave, pieces):
        return [
            lax.ppermute(piece, "dev", forward if ahead else backward)
            for (ahead, _), piece in zip(waves[wave], pieces)
        ]

    def marks_in(wave, pieces):
        return jnp.concatenate([marks_of(piece, t) for (_, t), piece in zip(waves[wave], pieces)])

    def products_of(wave, pieces):
        return products(pieces, marks_in(wave, pieces))

    def leaving(amps, ids, ranks):
        new, *rows_for = call(
            functools.partial(
                leaving_kernel, len(amps), ladder_slots, slots, len(parts), tiles, n_dev, n_grp, owned, ranks
            ),
            (sums(len(amps)),) + (sums(len(ranks)),) * (n_grp - 2),
            3,
            [ids, me, owners, *amps, ladder_panel, cycle_panel, *parts],
            rows_scratch,
        )
        return new, rows_for

    def core_sums(rows_for):
        return [
            rows_for[2 * k] + lax.ppermute(rows_for[2 * k + 1], "grp", swap) for k in range(len(shifts))
        ]

    def x_sums(chip):
        return [
            lax.ppermute(
                (rows * SCALE).astype(jnp.float16), "grp", [(g, (g + shift) % n_grp) for g in range(n_grp)]
            ).astype(jnp.float32)
            * (1 / SCALE)
            for shift, rows in zip(shifts, chip)
        ]

    def landed_after(parts, flying):
        landed = []
        for piece in flying:
            piece, parts = lax.optimization_barrier((piece, parts))
            landed.append(piece)
        return landed, parts

    first = hop(0, [own[t] for _, t in waves[0]])
    parts = [products(own, marks.reshape(-1))]
    own, parts = lax.optimization_barrier((own, parts))
    second = hop(1, [own[t] for _, t in waves[1]])
    for step in range(1, n_dev // 2):
        landed, parts = landed_after(parts, first)
        first = hop(0, landed)
        if step < n_dev // 2 - 1:
            parts.append(products_of(0, landed))
            landed, parts = landed_after(parts, second)
            second = hop(1, landed)
            parts.append(products_of(1, landed))
    n_soon = owned - tiles
    parts.append(products_of(0, landed))
    second, parts = lax.optimization_barrier((second, parts))
    parts = [jnp.concatenate(parts, axis=0)]
    new, rows_for = leaving(second, marks_in(1, second), range(n_soon))
    parts.append(new)
    soon = x_sums(core_sums(rows_for))
    new, rows_for = leaving(first, marks_in(0, first), range(n_soon, owned))
    parts.append(new)
    late = core_sums(rows_for)
    late, parts = lax.optimization_barrier((late, parts))
    late = x_sums(late)
    mine, partners = call(
        functools.partial(staying_kernel, len(parts), tiles, n_dev, owned),
        (sums(owned), sums(owned)),
        2,
        [me, owners, *parts],
    )
    got = lax.ppermute(partners, "grp", swap)
    return call(
        functools.partial(finish_kernel, tiles, n_dev, owned),
        jax.ShapeDtypeStruct(base.shape, base.dtype),
        2,
        [me, owners, base, mine, got, *(rows for pair in zip(soon, late) for rows in pair)],
    )


def solution(mesh):
    placed = (
        P("dev", "grp", None),
        P("dev", "grp"),
        P("dev", "grp"),
        P("dev", "grp", None),
        P("dev", "grp"),
        P("dev", "grp"),
        P("grp", "dev"),
        P("grp", "dev"),
        P(),
        P("grp", "dev"),
    )
    return jax.shard_map(
        per_device, mesh=mesh, in_specs=placed, out_specs=P("grp", "dev"), check_vma=False
    )
```

```python
import functools
import math

import jax
import jax.numpy as jnp
from jax import lax
from jax.experimental import pallas as pl
from jax.experimental.pallas import tpu as pltpu
from jax.sharding import PartitionSpec as P

TS = 64
HALF = TS // 2
LANES = 128
SCALE = 16.0
DEAD = 128
MARGIN = 1
VMEM = pl.BlockSpec(memory_space=pltpu.VMEM)
SMEM = pl.BlockSpec(memory_space=pltpu.SMEM)


def ring_order(n):
    return list(range(0, n, 2)) + list(range(n - 1, 0, -2))


def ring_place(d, n):
    return jnp.where(lax.rem(d, 2) == 0, lax.div(d, 2), n - 1 - lax.div(d, 2))


def rows_of(amps):
    tiles, slots, _ = amps.shape
    return amps.reshape(tiles, slots * HALF, 2 * TS)


def marked(ids, count):
    slot = jnp.arange(ids.shape[1], dtype=jnp.int32)[None, :]
    return jnp.where(slot < count, ids, ids + DEAD)


def multiply(ids_ref, amp_refs, ladder_ref, cycle_ref, ladder_slots, slots, rows_ref, out_ref):
    cols = ladder_ref.shape[1]
    for t, amp_ref in enumerate(amp_refs):
        total = jnp.zeros((TS, cols), jnp.float32)
        for q in range(0, slots, 4):
            left, right = [], []
            for s in range(q, min(q + 4, slots)):
                mark = ids_ref[t * slots + s]
                k = pl.multiple_of(lax.rem(mark, DEAD) * TS, TS)
                panel_ref = ladder_ref if s < ladder_slots else cycle_ref
                right.append(panel_ref[pl.ds(k, TS), :])
                tile = amp_ref[s * HALF : (s + 1) * HALF, :]
                tile = jnp.where(mark < DEAD, tile, jnp.zeros_like(tile))
                left.append(jnp.concatenate([tile[:, :TS], tile[:, TS:]], axis=0))
            total += jnp.dot(
                jnp.concatenate(left, axis=1),
                jnp.concatenate(right, axis=0),
                preferred_element_type=jnp.float32,
            )
        for c in range(cols // LANES):
            lanes = slice(c * LANES, (c + 1) * LANES)
            for part in range(2):
                rows_ref[t % 2, c, pl.ds(part, HALF, stride=2), :] = total[
                    part * HALF : (part + 1) * HALF, lanes
                ]
            out_ref[t * TS : (t + 1) * TS, lanes] = rows_ref[t % 2, c]


def arrival(row_tile, place, tiles, n_dev):
    t = lax.rem(row_tile, tiles)
    back = lax.rem(place - ring_place(lax.div(row_tile, tiles), n_dev) + n_dev, n_dev)
    half, cut = n_dev // 2, tiles // 2
    step = jnp.minimum(back, n_dev - back)
    there = jnp.where(back < half, jnp.where(t < cut, t, t + cut), jnp.where(t < cut, t + tiles + cut, t))
    slot = tiles + (step - 1) * 2 * tiles + jnp.where(back == half, t, there)
    return jnp.where(back == 0, t, slot)


def slots_of(group, owned, tiles, n_dev, owners_ref):
    place = ring_place(lax.axis_index("dev"), n_dev)
    slots = [arrival(owners_ref[group * owned + i], place, tiles, n_dev) for i in range(owned)]
    ranks = [sum((other < slot).astype(jnp.int32) for other in slots) for slot in slots]
    return list(zip(slots, ranks))


def tile_rows(ref, at):
    return ref.at[pl.ds(pl.multiple_of(at * TS, TS), TS), :]


def pick(part_refs, slot, out_ref, at):
    low = 0
    for part_ref in part_refs:
        high = low + part_ref.shape[0] // TS

        @pl.when((slot >= low) & (slot < high))
        def _():
            out_ref[at * TS : (at + 1) * TS, :] = tile_rows(part_ref, jnp.clip(slot - low, 0, high - low - 1))[...]

        low = high


def partner(group):
    return group + 1 - 2 * lax.rem(group, 2)


def tile_kernel(n, ladder_slots, slots, ids_ref, *refs):
    ladder_ref, cycle_ref, out_ref, rows_ref = refs[n:]
    multiply(ids_ref, refs[:n], ladder_ref, cycle_ref, ladder_slots, slots, rows_ref, out_ref)


def leaving_kernel(
    n, ladder_slots, slots, n_parts, tiles, n_dev, n_grp, owned, ranks, ids_ref, owners_ref, *refs
):
    amp_refs, (ladder_ref, cycle_ref), part_refs = refs[:n], refs[n : n + 2], refs[n + 2 :][:n_parts]
    new_ref, *out_refs, rows_ref = refs[n + 2 + n_parts :]
    multiply(ids_ref, amp_refs, ladder_ref, cycle_ref, ladder_slots, slots, rows_ref, new_ref)
    for k, shift in enumerate(range(2, n_grp, 2)):
        group = lax.rem(lax.axis_index("grp") + shift, n_grp)
        for owner, out_ref in zip((group, partner(group)), out_refs[2 * k :]):
            found = slots_of(owner, owned, tiles, n_dev, owners_ref)
            for at, wanted in enumerate(ranks):
                slot = sum(jnp.where(rank == wanted, slot, 0) for slot, rank in found)
                pick(part_refs + (new_ref,), slot, out_ref, at)


def staying_kernel(n_parts, tiles, n_dev, owned, owners_ref, *refs):
    part_refs, (mine_ref, partners_ref, rank_ref) = refs[:n_parts], refs[n_parts:]
    group = lax.axis_index("grp")
    for i, (slot, _) in enumerate(slots_of(partner(group), owned, tiles, n_dev, owners_ref)):
        pick(part_refs, slot, partners_ref, i)
    for i, (slot, rank) in enumerate(slots_of(group, owned, tiles, n_dev, owners_ref)):
        pick(part_refs, slot, mine_ref, i)
        rank_ref[i * TS : (i + 1) * TS, :] = jnp.full((TS, rank_ref.shape[1]), rank, jnp.int32)


def call(kernel, out_shape, n_smem, args, scratch=()):
    held = [*args, *jax.tree.leaves(out_shape)]
    held = sum(math.prod(x.shape) * x.dtype.itemsize for x in held)
    return pl.pallas_call(
        kernel,
        out_shape=out_shape,
        in_specs=[SMEM] * n_smem + [VMEM] * (len(args) - n_smem),
        out_specs=jax.tree.map(lambda _: VMEM, out_shape),
        scratch_shapes=list(scratch),
        compiler_params=pltpu.CompilerParams(vmem_limit_bytes=held + (MARGIN << 20)),
        cost_estimate=pl.CostEstimate(flops=1, bytes_accessed=1, transcendentals=0),
    )(*args)


def per_device(
    ladder_amps,
    ladder_ids,
    ladder_count,
    cycle_amps,
    cycle_ids,
    cycle_count,
    ladder_panel,
    cycle_panel,
    owners,
    base,
):
    n_dev, n_grp = lax.axis_size("dev"), lax.axis_size("grp")
    tiles, ladder_slots, _ = ladder_amps.shape
    slots = ladder_slots + cycle_amps.shape[1]
    order = ring_order(n_dev)
    forward = [(order[i], order[(i + 1) % n_dev]) for i in range(n_dev)]
    backward = [(b, a) for a, b in forward]
    swap = [(g, g ^ 1) for g in range(n_grp)]

    own = rows_of(jnp.concatenate([ladder_amps, cycle_amps], axis=1))
    own, ladder_ids, ladder_count, cycle_ids, cycle_count = lax.optimization_barrier(
        (own, ladder_ids, ladder_count, cycle_ids, cycle_count)
    )
    marks = jnp.concatenate(
        [marked(ladder_ids, ladder_count), marked(cycle_ids, cycle_count)], axis=1
    )
    marks = jnp.concatenate([marks[t : t + 1] for t in range(tiles)], axis=1)
    note = jnp.pad(marks.astype(jnp.bfloat16), ((0, 7), (0, 2 * TS - marks.size)))
    own = [jnp.concatenate([own[t], note], axis=0) for t in range(tiles)]

    def marks_of(piece, t):
        return piece[slots * HALF, t * slots : (t + 1) * slots].astype(jnp.int32)

    cols = base.shape[1]
    rows_scratch = [pltpu.VMEM((2, cols // LANES, TS, LANES), jnp.float32)]

    def products(amps, ids):
        return call(
            functools.partial(tile_kernel, len(amps), ladder_slots, slots),
            jax.ShapeDtypeStruct((len(amps) * TS, cols), jnp.float32),
            1,
            [ids, *amps, ladder_panel, cycle_panel],
            rows_scratch,
        )

    owned = owners.shape[0] // n_grp
    shifts = range(2, n_grp, 2)

    def sums(n):
        return jax.ShapeDtypeStruct((n * TS, cols), jnp.float32)

    cut = tiles // 2
    waves = [
        [(t < cut, t) for t in range(tiles)],
        [(t >= cut, t) for t in (*range(cut, tiles), *range(cut))],
    ]

    def hop(wave, pieces):
        return [
            lax.ppermute(piece, "dev", forward if ahead else backward)
            for (ahead, _), piece in zip(waves[wave], pieces)
        ]

    def marks_in(wave, pieces):
        return jnp.concatenate([marks_of(piece, t) for (_, t), piece in zip(waves[wave], pieces)])

    def products_of(wave, pieces):
        return products(pieces, marks_in(wave, pieces))

    def leaving(amps, ids, ranks):
        new, *rows_for = call(
            functools.partial(
                leaving_kernel, len(amps), ladder_slots, slots, len(parts), tiles, n_dev, n_grp, owned, ranks
            ),
            (sums(len(amps)),) + (sums(len(ranks)),) * (n_grp - 2),
            2,
            [ids, owners, *amps, ladder_panel, cycle_panel, *parts],
            rows_scratch,
        )
        return new, rows_for

    def core_sums(rows_for):
        return [
            rows_for[2 * k] + lax.ppermute(rows_for[2 * k + 1], "grp", swap) for k in range(len(shifts))
        ]

    def sent(chip):
        return [
            lax.ppermute(
                (rows * SCALE).astype(jnp.float16), "grp", [(g, (g + shift) % n_grp) for g in range(n_grp)]
            )
            for shift, rows in zip(shifts, chip)
        ]

    def landed_after(parts, flying):
        landed = []
        for piece in flying:
            piece, parts = lax.optimization_barrier((piece, parts))
            landed.append(piece)
        return landed, parts

    first = hop(0, [own[t] for _, t in waves[0]])
    parts = [products(own, marks_in(0, own))]
    own, parts = lax.optimization_barrier((own, parts))
    second = hop(1, [own[t] for _, t in waves[1]])
    for step in range(1, n_dev // 2):
        landed, parts = landed_after(parts, first)
        first = hop(0, landed)
        if step < n_dev // 2 - 1:
            parts.append(products_of(0, landed))
            landed, parts = landed_after(parts, second)
            second = hop(1, landed)
            parts.append(products_of(1, landed))
    n_soon = owned - tiles
    parts.append(products_of(0, landed))
    parts = [jnp.concatenate(parts, axis=0)]
    second, parts = lax.optimization_barrier((second, parts))
    new, rows_for = leaving(second, marks_in(1, second), range(n_soon))
    parts.append(new)
    soon = sent(core_sums(rows_for))
    new, rows_for = leaving(first, marks_in(0, first), range(n_soon, owned))
    parts.append(new)
    late = core_sums(rows_for)
    late, parts = lax.optimization_barrier((late, parts))
    late = sent(late)
    mine, partners, rank = call(
        functools.partial(staying_kernel, len(parts), tiles, n_dev, owned),
        (sums(owned), sums(owned), jax.ShapeDtypeStruct((owned * TS, cols), jnp.int32)),
        1,
        [owners, *parts],
    )
    total = base + (mine + lax.ppermute(partners, "grp", swap))
    rank = rank.reshape(owned, TS, cols)
    for rows in zip(soon, late):
        rows = [part.reshape(1, -1, TS, cols)[:, k] for part in rows for k in range(part.shape[0] // TS)]
        chosen = rows[0]
        for k in range(1, owned):
            chosen = jnp.where(rank == k, rows[k], chosen)
        chosen = chosen.astype(jnp.float32) * (1 / SCALE)
        total = total + chosen.reshape(base.shape)
    return total


def solution(mesh):
    placed = (
        P("dev", "grp", None),
        P("dev", "grp"),
        P("dev", "grp"),
        P("dev", "grp", None),
        P("dev", "grp"),
        P("dev", "grp"),
        P("grp", "dev"),
        P("grp", "dev"),
        P(),
        P("grp", "dev"),
    )
    return jax.shard_map(
        per_device, mesh=mesh, in_specs=placed, out_specs=P("grp", "dev"), check_vma=False
    )
```

```python
import functools
import math

import jax
import jax.numpy as jnp
from jax import lax
from jax.experimental import pallas as pl
from jax.experimental.pallas import tpu as pltpu
from jax.sharding import PartitionSpec as P

TS = 64
HALF = TS // 2
LANES = 128
SCALE = 16.0
DEAD = 128
MARGIN = 1
VMEM = pl.BlockSpec(memory_space=pltpu.VMEM)
SMEM = pl.BlockSpec(memory_space=pltpu.SMEM)


def remainder(x, n):
    return lax.rem(x, n) if n & (n - 1) else x & (n - 1)


def quotient(x, n):
    return lax.div(x, n) if n & (n - 1) else x >> (n.bit_length() - 1)


def ring_order(n):
    return list(range(0, n, 2)) + list(range(n - 1, 0, -2))


def ring_place(d, n):
    return jnp.where(remainder(d, 2) == 0, quotient(d, 2), n - 1 - quotient(d, 2))


def rows_of(amps):
    tiles, slots, _ = amps.shape
    return amps.reshape(tiles, slots * HALF, 2 * TS)


def marked(ids, count):
    slot = jnp.arange(ids.shape[1], dtype=jnp.int32)[None, :]
    return jnp.where(slot < count, ids, ids + DEAD)


def multiply(ids_ref, amp_refs, ladder_ref, cycle_ref, ladder_slots, slots, rows_ref, out_ref):
    cols = ladder_ref.shape[1]
    for t, amp_ref in enumerate(amp_refs):
        total = jnp.zeros((TS, cols), jnp.float32)
        for q in range(0, slots, 4):
            left, right = [], []
            for s in range(q, min(q + 4, slots)):
                mark = ids_ref[t * slots + s]
                k = pl.multiple_of(remainder(mark, DEAD) * TS, TS)
                panel_ref = ladder_ref if s < ladder_slots else cycle_ref
                right.append(panel_ref[pl.ds(k, TS), :])
                tile = amp_ref[s * HALF : (s + 1) * HALF, :]
                tile = jnp.where(mark < DEAD, tile, jnp.zeros_like(tile))
                left.append(jnp.concatenate([tile[:, :TS], tile[:, TS:]], axis=0))
            total += jnp.dot(
                jnp.concatenate(left, axis=1),
                jnp.concatenate(right, axis=0),
                preferred_element_type=jnp.float32,
            )
        for c in range(cols // LANES):
            lanes = slice(c * LANES, (c + 1) * LANES)
            for part in range(2):
                rows_ref[t % 2, c, pl.ds(part, HALF, stride=2), :] = total[
                    part * HALF : (part + 1) * HALF, lanes
                ]
            out_ref[t * TS : (t + 1) * TS, lanes] = rows_ref[t % 2, c]


def arrival(row_tile, place, tiles, n_dev):
    t = remainder(row_tile, tiles)
    back = remainder(place - ring_place(quotient(row_tile, tiles), n_dev) + n_dev, n_dev)
    half, cut = n_dev // 2, tiles // 2
    step = jnp.minimum(back, n_dev - back)
    there = jnp.where(back < half, jnp.where(t < cut, t, t + cut), jnp.where(t < cut, t + tiles + cut, t))
    slot = tiles + (step - 1) * 2 * tiles + jnp.where(back == half, t, there)
    return jnp.where(back == 0, t, slot)


def slots_of(group, owned, tiles, n_dev, owners_ref):
    place = ring_place(lax.axis_index("dev"), n_dev)
    slots = [arrival(owners_ref[group * owned + i], place, tiles, n_dev) for i in range(owned)]
    ranks = [sum((other < slot).astype(jnp.int32) for other in slots) for slot in slots]
    return list(zip(slots, ranks))


def tile_rows(ref, at):
    return ref.at[pl.ds(pl.multiple_of(at * TS, TS), TS), :]


def pick(part_refs, slot, out_ref, at):
    low = 0
    for part_ref in part_refs:
        high = low + part_ref.shape[0] // TS

        @pl.when((slot >= low) & (slot < high))
        def _():
            out_ref[at * TS : (at + 1) * TS, :] = tile_rows(part_ref, jnp.clip(slot - low, 0, high - low - 1))[...]

        low = high


def partner(group):
    return group + 1 - 2 * remainder(group, 2)


def tile_kernel(n, ladder_slots, slots, ids_ref, *refs):
    ladder_ref, cycle_ref, out_ref, rows_ref = refs[n:]
    multiply(ids_ref, refs[:n], ladder_ref, cycle_ref, ladder_slots, slots, rows_ref, out_ref)


def leaving_kernel(
    n, ladder_slots, slots, n_parts, tiles, n_dev, n_grp, owned, ranks, ids_ref, owners_ref, *refs
):
    amp_refs, (ladder_ref, cycle_ref), part_refs = refs[:n], refs[n : n + 2], refs[n + 2 :][:n_parts]
    new_ref, *out_refs, rows_ref = refs[n + 2 + n_parts :]
    multiply(ids_ref, amp_refs, ladder_ref, cycle_ref, ladder_slots, slots, rows_ref, new_ref)
    for k, shift in enumerate(range(2, n_grp, 2)):
        group = remainder(lax.axis_index("grp") + shift, n_grp)
        for owner, out_ref in zip((group, partner(group)), out_refs[2 * k :]):
            found = slots_of(owner, owned, tiles, n_dev, owners_ref)
            for at, wanted in enumerate(ranks):
                slot = sum(jnp.where(rank == wanted, slot, 0) for slot, rank in found)
                pick(part_refs + (new_ref,), slot, out_ref, at)


def staying_kernel(n_parts, tiles, n_dev, owned, owners_ref, *refs):
    part_refs, (mine_ref, partners_ref, rank_ref) = refs[:n_parts], refs[n_parts:]
    group = lax.axis_index("grp")
    for i, (slot, _) in enumerate(slots_of(partner(group), owned, tiles, n_dev, owners_ref)):
        pick(part_refs, slot, partners_ref, i)
    for i, (slot, rank) in enumerate(slots_of(group, owned, tiles, n_dev, owners_ref)):
        pick(part_refs, slot, mine_ref, i)
        rank_ref[i * TS : (i + 1) * TS, :] = jnp.full((TS, rank_ref.shape[1]), rank, jnp.int32)


def call(kernel, out_shape, n_smem, args, scratch=()):
    held = [*args, *jax.tree.leaves(out_shape)]
    held = sum(math.prod(x.shape) * x.dtype.itemsize for x in held)
    return pl.pallas_call(
        kernel,
        out_shape=out_shape,
        in_specs=[SMEM] * n_smem + [VMEM] * (len(args) - n_smem),
        out_specs=jax.tree.map(lambda _: VMEM, out_shape),
        scratch_shapes=list(scratch),
        compiler_params=pltpu.CompilerParams(vmem_limit_bytes=held + (MARGIN << 20)),
        cost_estimate=pl.CostEstimate(flops=1, bytes_accessed=1, transcendentals=0),
    )(*args)


def per_device(
    ladder_amps,
    ladder_ids,
    ladder_count,
    cycle_amps,
    cycle_ids,
    cycle_count,
    ladder_panel,
    cycle_panel,
    owners,
    base,
):
    n_dev, n_grp = lax.axis_size("dev"), lax.axis_size("grp")
    tiles, ladder_slots, _ = ladder_amps.shape
    slots = ladder_slots + cycle_amps.shape[1]
    order = ring_order(n_dev)
    forward = [(order[i], order[(i + 1) % n_dev]) for i in range(n_dev)]
    backward = [(b, a) for a, b in forward]
    swap = [(g, g ^ 1) for g in range(n_grp)]

    own = rows_of(jnp.concatenate([ladder_amps, cycle_amps], axis=1))
    own, ladder_ids, ladder_count, cycle_ids, cycle_count = lax.optimization_barrier(
        (own, ladder_ids, ladder_count, cycle_ids, cycle_count)
    )
    slot = jnp.arange(slots, dtype=jnp.int32)[None, :]
    ids = jnp.concatenate([ladder_ids, cycle_ids], axis=1)
    live = jnp.where(slot < ladder_slots, slot < ladder_count, slot - ladder_slots < cycle_count)
    marks = jnp.where(live, ids, ids + DEAD)
    marks = jnp.concatenate([marks[t : t + 1] for t in range(tiles)], axis=1)
    note = jnp.pad(marks.astype(jnp.bfloat16), ((0, 7), (0, 2 * TS - marks.size)))
    own = [jnp.concatenate([own[t], note], axis=0) for t in range(tiles)]

    def marks_of(piece, t):
        return piece[slots * HALF, t * slots : (t + 1) * slots].astype(jnp.int32)

    cols = base.shape[1]
    rows_scratch = [pltpu.VMEM((2, cols // LANES, TS, LANES), jnp.float32)]

    def products(amps, ids):
        return call(
            functools.partial(tile_kernel, len(amps), ladder_slots, slots),
            jax.ShapeDtypeStruct((len(amps) * TS, cols), jnp.float32),
            1,
            [ids, *amps, ladder_panel, cycle_panel],
            rows_scratch,
        )

    owned = owners.shape[0] // n_grp
    shifts = range(2, n_grp, 2)

    def sums(n):
        return jax.ShapeDtypeStruct((n * TS, cols), jnp.float32)

    cut = tiles // 2
    waves = [
        [(t < cut, t) for t in range(tiles)],
        [(t >= cut, t) for t in (*range(cut, tiles), *range(cut))],
    ]

    def hop(wave, pieces):
        return [
            lax.ppermute(piece, "dev", forward if ahead else backward)
            for (ahead, _), piece in zip(waves[wave], pieces)
        ]

    def marks_in(wave, pieces):
        return jnp.concatenate([marks_of(piece, t) for (_, t), piece in zip(waves[wave], pieces)])

    def products_of(wave, pieces):
        return products(pieces, marks_in(wave, pieces))

    def leaving(amps, ids, ranks):
        new, *rows_for = call(
            functools.partial(
                leaving_kernel, len(amps), ladder_slots, slots, len(parts), tiles, n_dev, n_grp, owned, ranks
            ),
            (sums(len(amps)),) + (sums(len(ranks)),) * (n_grp - 2),
            2,
            [ids, owners, *amps, ladder_panel, cycle_panel, *parts],
            rows_scratch,
        )
        return new, rows_for

    def core_sums(rows_for):
        return [
            rows_for[2 * k] + lax.ppermute(rows_for[2 * k + 1], "grp", swap) for k in range(len(shifts))
        ]

    def sent(chip):
        return [
            lax.ppermute(
                (rows * SCALE).astype(jnp.float16), "grp", [(g, (g + shift) % n_grp) for g in range(n_grp)]
            )
            for shift, rows in zip(shifts, chip)
        ]

    def landed_after(parts, flying):
        landed = []
        for piece in flying:
            piece, parts = lax.optimization_barrier((piece, parts))
            landed.append(piece)
        return landed, parts

    first = hop(0, [own[t] for _, t in waves[0]])
    parts = [products(own, marks_in(0, own))]
    own, parts = lax.optimization_barrier((own, parts))
    second = hop(1, [own[t] for _, t in waves[1]])
    for step in range(1, n_dev // 2):
        landed, parts = landed_after(parts, first)
        first = hop(0, landed)
        if step < n_dev // 2 - 1:
            parts.append(products_of(0, landed))
            landed, parts = landed_after(parts, second)
            second = hop(1, landed)
            parts.append(products_of(1, landed))
    n_soon = owned - tiles
    parts.append(products_of(0, landed))
    parts = [jnp.concatenate(parts, axis=0)]
    second, parts = lax.optimization_barrier((second, parts))
    new, rows_for = leaving(second, marks_in(1, second), range(n_soon))
    parts.append(new)
    soon = sent(core_sums(rows_for))
    new, rows_for = leaving(first, marks_in(0, first), range(n_soon, owned))
    parts.append(new)
    late = core_sums(rows_for)
    late, parts = lax.optimization_barrier((late, parts))
    late = sent(late)
    mine, partners, rank = call(
        functools.partial(staying_kernel, len(parts), tiles, n_dev, owned),
        (sums(owned), sums(owned), jax.ShapeDtypeStruct((owned * TS, cols), jnp.int32)),
        1,
        [owners, *parts],
    )
    total = base + (mine + lax.ppermute(partners, "grp", swap))
    rank = rank.reshape(owned, TS, cols)
    for rows in zip(soon, late):
        rows = [part.reshape(1, -1, TS, cols)[:, k] for part in rows for k in range(part.shape[0] // TS)]
        chosen = rows[0]
        for k in range(1, owned):
            chosen = jnp.where(rank == k, rows[k], chosen)
        chosen = chosen.astype(jnp.float32) * (1 / SCALE)
        total = total + chosen.reshape(base.shape)
    return total


def solution(mesh):
    placed = (
        P("dev", "grp", None),
        P("dev", "grp"),
        P("dev", "grp"),
        P("dev", "grp", None),
        P("dev", "grp"),
        P("dev", "grp"),
        P("grp", "dev"),
        P("grp", "dev"),
        P(),
        P("grp", "dev"),
    )
    return jax.shard_map(
        per_device, mesh=mesh, in_specs=placed, out_specs=P("grp", "dev"), check_vma=False
    )
```

```python
import functools
import math

import jax
import jax.numpy as jnp
from jax import lax
from jax.experimental import pallas as pl
from jax.experimental.pallas import tpu as pltpu
from jax.sharding import PartitionSpec as P

TS = 64
HALF = TS // 2
LANES = 128
SCALE = 16.0
DEAD = 128
MARGIN = 1
VMEM = pl.BlockSpec(memory_space=pltpu.VMEM)
SMEM = pl.BlockSpec(memory_space=pltpu.SMEM)


def remainder(x, n):
    return lax.rem(x, n) if n & (n - 1) else x & (n - 1)


def quotient(x, n):
    return lax.div(x, n) if n & (n - 1) else x >> (n.bit_length() - 1)


def ring_order(n):
    return list(range(0, n, 2)) + list(range(n - 1, 0, -2))


def ring_place(d, n):
    return jnp.where(remainder(d, 2) == 0, quotient(d, 2), n - 1 - quotient(d, 2))


def rows_of(amps):
    tiles, slots, _ = amps.shape
    return amps.reshape(tiles, slots * HALF, 2 * TS)


def marked(ids, count):
    slot = jnp.arange(ids.shape[1], dtype=jnp.int32)[None, :]
    return jnp.where(slot < count, ids, ids + DEAD)


def multiply(ids_ref, amp_refs, ladder_ref, cycle_ref, ladder_slots, slots, rows_ref, out_ref):
    cols = ladder_ref.shape[1]
    for t, amp_ref in enumerate(amp_refs):
        total = jnp.zeros((TS, cols), jnp.float32)
        for q in range(0, slots, 4):
            left, right = [], []
            for s in range(q, min(q + 4, slots)):
                mark = ids_ref[t * slots + s]
                k = pl.multiple_of(remainder(mark, DEAD) * TS, TS)
                panel_ref = ladder_ref if s < ladder_slots else cycle_ref
                right.append(panel_ref[pl.ds(k, TS), :])
                tile = amp_ref[s * HALF : (s + 1) * HALF, :]
                tile = jnp.where(mark < DEAD, tile, jnp.zeros_like(tile))
                left.append(jnp.concatenate([tile[:, :TS], tile[:, TS:]], axis=0))
            total += jnp.dot(
                jnp.concatenate(left, axis=1),
                jnp.concatenate(right, axis=0),
                preferred_element_type=jnp.float32,
            )
        for c in range(cols // LANES):
            lanes = slice(c * LANES, (c + 1) * LANES)
            for part in range(2):
                rows_ref[t % 2, c, pl.ds(part, HALF, stride=2), :] = total[
                    part * HALF : (part + 1) * HALF, lanes
                ]
            out_ref[t * TS : (t + 1) * TS, lanes] = rows_ref[t % 2, c]


def arrival(row_tile, place, tiles, n_dev):
    t = remainder(row_tile, tiles)
    back = remainder(place - ring_place(quotient(row_tile, tiles), n_dev) + n_dev, n_dev)
    half, cut = n_dev // 2, tiles // 2
    step = jnp.minimum(back, n_dev - back)
    there = jnp.where(back < half, jnp.where(t < cut, t, t + cut), jnp.where(t < cut, t + tiles + cut, t))
    slot = tiles + (step - 1) * 2 * tiles + jnp.where(back == half, t, there)
    return jnp.where(back == 0, t, slot)


def slots_of(group, owned, tiles, n_dev, owners_ref):
    place = ring_place(lax.axis_index("dev"), n_dev)
    slots = [arrival(owners_ref[group * owned + i], place, tiles, n_dev) for i in range(owned)]
    ranks = [sum((other < slot).astype(jnp.int32) for other in slots) for slot in slots]
    return list(zip(slots, ranks))


def tile_rows(ref, at):
    return ref.at[pl.ds(pl.multiple_of(at * TS, TS), TS), :]


def pick(part_refs, slot, out_ref, at):
    low = 0
    for part_ref in part_refs:
        high = low + part_ref.shape[0] // TS

        @pl.when((slot >= low) & (slot < high))
        def _():
            out_ref[at * TS : (at + 1) * TS, :] = tile_rows(part_ref, jnp.clip(slot - low, 0, high - low - 1))[...]

        low = high


def partner(group):
    return group + 1 - 2 * remainder(group, 2)


def tile_kernel(n, ladder_slots, slots, ids_ref, *refs):
    ladder_ref, cycle_ref, out_ref, rows_ref = refs[n:]
    multiply(ids_ref, refs[:n], ladder_ref, cycle_ref, ladder_slots, slots, rows_ref, out_ref)


def leaving_kernel(
    n, ladder_slots, slots, n_parts, tiles, n_dev, n_grp, owned, ranks, ids_ref, owners_ref, *refs
):
    amp_refs, (ladder_ref, cycle_ref), part_refs = refs[:n], refs[n : n + 2], refs[n + 2 :][:n_parts]
    new_ref, *out_refs, rows_ref = refs[n + 2 + n_parts :]
    multiply(ids_ref, amp_refs, ladder_ref, cycle_ref, ladder_slots, slots, rows_ref, new_ref)
    for k, shift in enumerate(range(2, n_grp, 2)):
        group = remainder(lax.axis_index("grp") + shift, n_grp)
        for owner, out_ref in zip((group, partner(group)), out_refs[2 * k :]):
            found = slots_of(owner, owned, tiles, n_dev, owners_ref)
            for at, wanted in enumerate(ranks):
                slot = sum(jnp.where(rank == wanted, slot, 0) for slot, rank in found)
                pick(part_refs + (new_ref,), slot, out_ref, at)


def staying_kernel(n_parts, tiles, n_dev, owned, owners_ref, *refs):
    part_refs, (mine_ref, partners_ref, rank_ref) = refs[:n_parts], refs[n_parts:]
    group = lax.axis_index("grp")
    for i, (slot, _) in enumerate(slots_of(partner(group), owned, tiles, n_dev, owners_ref)):
        pick(part_refs, slot, partners_ref, i)
    for i, (slot, rank) in enumerate(slots_of(group, owned, tiles, n_dev, owners_ref)):
        pick(part_refs, slot, mine_ref, i)
        rank_ref[i * TS : (i + 1) * TS, :] = jnp.full((TS, rank_ref.shape[1]), rank, jnp.int32)


def call(kernel, out_shape, n_smem, args, scratch=()):
    held = [*args, *jax.tree.leaves(out_shape)]
    held = sum(math.prod(x.shape) * x.dtype.itemsize for x in held)
    return pl.pallas_call(
        kernel,
        out_shape=out_shape,
        in_specs=[SMEM] * n_smem + [VMEM] * (len(args) - n_smem),
        out_specs=jax.tree.map(lambda _: VMEM, out_shape),
        scratch_shapes=list(scratch),
        compiler_params=pltpu.CompilerParams(vmem_limit_bytes=held + (MARGIN << 20)),
        cost_estimate=pl.CostEstimate(flops=1, bytes_accessed=1, transcendentals=0),
    )(*args)


def per_device(
    ladder_amps,
    ladder_ids,
    ladder_count,
    cycle_amps,
    cycle_ids,
    cycle_count,
    ladder_panel,
    cycle_panel,
    owners,
    base,
):
    n_dev, n_grp = lax.axis_size("dev"), lax.axis_size("grp")
    tiles, ladder_slots, _ = ladder_amps.shape
    slots = ladder_slots + cycle_amps.shape[1]
    order = ring_order(n_dev)
    forward = [(order[i], order[(i + 1) % n_dev]) for i in range(n_dev)]
    backward = [(b, a) for a, b in forward]
    swap = [(g, g ^ 1) for g in range(n_grp)]

    own = rows_of(jnp.concatenate([ladder_amps, cycle_amps], axis=1))
    own, ladder_ids, ladder_count, cycle_ids, cycle_count = lax.optimization_barrier(
        (own, ladder_ids, ladder_count, cycle_ids, cycle_count)
    )
    slot = jnp.arange(slots, dtype=jnp.int32)[None, :]
    ids = jnp.concatenate([ladder_ids, cycle_ids], axis=1)
    live = jnp.where(slot < ladder_slots, slot < ladder_count, slot - ladder_slots < cycle_count)
    marks = jnp.where(live, ids, ids + DEAD)
    marks = jnp.concatenate([marks[t : t + 1] for t in range(tiles)], axis=1)
    note = jnp.pad(marks.astype(jnp.bfloat16), ((0, 7), (0, 2 * TS - marks.size)))
    own = [jnp.concatenate([own[t], note], axis=0) for t in range(tiles)]

    def marks_of(piece, t):
        return piece[slots * HALF, t * slots : (t + 1) * slots].astype(jnp.int32)

    cols = base.shape[1]
    rows_scratch = [pltpu.VMEM((2, cols // LANES, TS, LANES), jnp.float32)]

    def products(amps, ids):
        return call(
            functools.partial(tile_kernel, len(amps), ladder_slots, slots),
            jax.ShapeDtypeStruct((len(amps) * TS, cols), jnp.float32),
            1,
            [ids, *amps, ladder_panel, cycle_panel],
            rows_scratch,
        )

    owned = owners.shape[0] // n_grp
    shifts = range(2, n_grp, 2)

    def sums(n):
        return jax.ShapeDtypeStruct((n * TS, cols), jnp.float32)

    cut = tiles // 2
    waves = [
        [(t < cut, t) for t in range(tiles)],
        [(t >= cut, t) for t in (*range(cut, tiles), *range(cut))],
    ]

    def hop(wave, pieces):
        return [
            lax.ppermute(piece, "dev", forward if ahead else backward)
            for (ahead, _), piece in zip(waves[wave], pieces)
        ]

    def marks_in(wave, pieces):
        return jnp.concatenate([marks_of(piece, t) for (_, t), piece in zip(waves[wave], pieces)])

    def products_of(wave, pieces):
        return products(pieces, marks_in(wave, pieces))

    def leaving(amps, ids, ranks):
        new, *rows_for = call(
            functools.partial(
                leaving_kernel, len(amps), ladder_slots, slots, len(parts), tiles, n_dev, n_grp, owned, ranks
            ),
            (sums(len(amps)),) + (sums(len(ranks)),) * (n_grp - 2),
            2,
            [ids, owners, *amps, ladder_panel, cycle_panel, *parts],
            rows_scratch,
        )
        return new, rows_for

    def core_sums(rows_for):
        return [
            rows_for[2 * k] + lax.ppermute(rows_for[2 * k + 1], "grp", swap) for k in range(len(shifts))
        ]

    def sent(chip):
        return [
            lax.ppermute(
                (rows * SCALE).astype(jnp.float16), "grp", [(g, (g + shift) % n_grp) for g in range(n_grp)]
            )
            for shift, rows in zip(shifts, chip)
        ]

    def landed_after(parts, flying):
        landed = []
        for piece in flying:
            piece, parts = lax.optimization_barrier((piece, parts))
            landed.append(piece)
        return landed, parts

    first = hop(0, [own[t] for _, t in waves[0]])
    parts = [products(own, marks_in(0, own))]
    second = hop(1, [own[t] for _, t in waves[1]])
    for step in range(1, n_dev // 2):
        landed, parts = landed_after(parts, first)
        first = hop(0, landed)
        if step < n_dev // 2 - 1:
            parts.append(products_of(0, landed))
            landed, parts = landed_after(parts, second)
            second = hop(1, landed)
            parts.append(products_of(1, landed))
    n_soon = owned - tiles
    parts.append(products_of(0, landed))
    parts = [jnp.concatenate(parts, axis=0)]
    second, parts = lax.optimization_barrier((second, parts))
    new, rows_for = leaving(second, marks_in(1, second), range(n_soon))
    parts.append(new)
    soon = sent(core_sums(rows_for))
    new, rows_for = leaving(first, marks_in(0, first), range(n_soon, owned))
    parts.append(new)
    late = core_sums(rows_for)
    late, parts = lax.optimization_barrier((late, parts))
    late = sent(late)
    mine, partners, rank = call(
        functools.partial(staying_kernel, len(parts), tiles, n_dev, owned),
        (sums(owned), sums(owned), jax.ShapeDtypeStruct((owned * TS, cols), jnp.int32)),
        1,
        [owners, *parts],
    )
    total = base + (mine + lax.ppermute(partners, "grp", swap))
    rank = rank.reshape(owned, TS, cols)
    for rows in zip(soon, late):
        rows = [part.reshape(1, -1, TS, cols)[:, k] for part in rows for k in range(part.shape[0] // TS)]
        chosen = rows[0]
        for k in range(1, owned):
            chosen = jnp.where(rank == k, rows[k], chosen)
        chosen = chosen.astype(jnp.float32) * (1 / SCALE)
        total = total + chosen.reshape(base.shape)
    return total


def solution(mesh):
    placed = (
        P("dev", "grp", None),
        P("dev", "grp"),
        P("dev", "grp"),
        P("dev", "grp", None),
        P("dev", "grp"),
        P("dev", "grp"),
        P("grp", "dev"),
        P("grp", "dev"),
        P(),
        P("grp", "dev"),
    )
    return jax.shard_map(
        per_device, mesh=mesh, in_specs=placed, out_specs=P("grp", "dev"), check_vma=False
    )
```
